512 devices in a mesh: section: 64 (over x, y, z_hi, core), tp: 8 (over z_lo).
Axes of the slice: x: 4, y: 4, z: 16 (z_hi: 2, z_lo: 8; z = z_hi * 8 + z_lo), core: 2. Of those that a mesh axis runs over, the one named last changes fastest.
Arguments:
- queries: bfloat16 [64, 128, 8192], P('section', None, 'tp')
- fresh_kv: bfloat16 [64, 128, 2048], P('section', 'tp'), may hold values from -6 to 6
- pool_kv: bfloat16 [64, 32, 64, 2048], P('section', None, None, 'tp'), may hold values from -6 to 6
- hit_pages: int32 [64, 64], P('section'), may hold values from 0 to 31
- hit_owners: int32 [64, 64, 1], P('section'), may hold values from 0 to 63; in each aligned block of 64 rows (0 to 63, 64 to 127, ..., all dimensions but the last counted through in order) at most 2 rows name the same one
- offsets: int32 [64], P('section'), may hold values from 64 to 4096
Outputs:
- attended: bfloat16 [64, 128, 8192], P('section', None, 'tp')
The draws below stay inside these ranges and needn't reach their ends.
Inputs may be any that keep to these rules, and one draw needn't show every extreme that they name: `hit_owners`: within the list of one layer no owner appears more than 2 times, and some owner appears exactly 2 times.
All inputs are finite; a program needn't handle non-finite values.
Results may differ from the reference program's by a relative error of at most 0.003.
Values may be sent and summed in bfloat16 or wider, within the bound.
A program may use at most 64 MiB of HBM per device.

```python
import math
import jax
import jax.numpy as jnp
import numpy as np
from jax import lax

HEAD = 128
QPK = 8
KVH = 8
QH = 64
LAYERS = 64
OWNERS = 64
SPAN = 128
HITS = 64
PAGE = 64
POOL = 32
MOST = 2
N_SECTION = 64


def draw_queries(key, part):
    key = jax.random.fold_in(key, 7)
    shape = (LAYERS, SPAN, QH * HEAD)
    base = jnp.clip(jax.random.normal(key, shape, jnp.float32), -6.0, 6.0) * 3.0
    return base.astype(jnp.bfloat16)


def plant(array, stream_key, low, largest):
    extent = array.shape
    place = [jax.random.randint(jax.random.fold_in(stream_key, axis), (), 0, extent[axis]) for axis in range(len(extent))]
    array = array.at[tuple(place)].set(low)
    longest = extent.index(max(extent))
    place[longest] = (place[longest] + 1) % extent[longest]
    return array.at[tuple(place)].set(largest)


def block_scale(rng, shape, cuts, least, largest):
    level, own = 1.0, jax.random.fold_in(rng, 6)
    for axis_at, blocks in cuts:
        heights = jnp.exp(jax.random.uniform(jax.random.fold_in(own, axis_at), (blocks,), jnp.float32, least / len(cuts), largest / len(cuts)))
        level = level * jnp.repeat(heights, shape[axis_at] // blocks).reshape([-1 if axis == axis_at else 1 for axis in range(len(shape))])
    return level


def shared_out(rng, own, number, rows, count, top, bound, lean):
    sequence = jax.random.permutation(rng, count)
    heavy_load, ordinary = load_shares(count, rows * top, bound, lean, True), load_shares(count, rows * top, bound, lean, False)
    places = jnp.arange(count)

    def named(sizes, rotation):
        used = int((sizes > 0).sum())
        fixed = max(1, used // 4)
        moved = fixed + (places - fixed + rotation * (used - fixed)) % max(1, count - fixed)
        return jnp.zeros((count,), jnp.int32).at[sequence[jnp.where(places < fixed, places, moved)]].set(jnp.asarray(sizes, jnp.int32))

    sizes = jnp.where(number % 4 == 0, named(heavy_load, number // 4), named(ordinary, number - number // 4 - 1))
    mixed = jax.random.permutation(jax.random.fold_in(own, 3), count)
    giver, taker = mixed[0:count // 2 * 2:2], mixed[1:count // 2 * 2:2]
    room = jnp.minimum(sizes[giver] - 1, bound - sizes[taker]) // 2
    room = jnp.where((giver == sequence[0]) | (taker == sequence[0]) | (sizes[taker] == 0), 0, jnp.maximum(room, 0))
    moved = jax.random.randint(jax.random.fold_in(own, 4), (count // 2,), 0, 1 << 20) % (room + 1)
    sizes = sizes.at[giver].add(-moved).at[taker].add(moved)
    labels = jnp.searchsorted(jnp.cumsum(sizes), jnp.arange(rows * top), side="right").astype(jnp.int32)
    table = labels.reshape(top, rows).T
    table = table[jax.random.permutation(jax.random.fold_in(own, 1), rows)]
    rotation = jax.random.randint(jax.random.fold_in(own, 2), (rows, 1), 0, top)
    return jnp.take_along_axis(table, (jnp.arange(top)[None, :] + rotation) % top, axis=1)


def load_shares(count, total, limit, slope, full):
    weights = [(1 << 20) // math.isqrt(rank ** slope) + 1 for rank in range(1, count + 1)]
    largest = limit if full else min(limit, max(-(-total // count), total * weights[0] // sum(weights)))
    least = 1 if total - largest >= count - 1 else 0
    given, rest = [largest] + [least] * (count - 1), total - largest - least * (count - 1)
    while rest > 0:
        free = [i for i in range(1, count) if given[i] < largest] or [i for i in range(1, count) if given[i] < limit]
        mass, remaining = sum([weights[i] for i in free]), rest
        for i in free:
            more = min(limit - given[i], max(1, remaining * weights[i] // mass), rest)
            given[i] = given[i] + more
            rest = rest - more
    return np.array(given)


def bell_draw(key, shape, deviation, limit, split=(), kind=jnp.bfloat16):
    values = deviation * jax.random.normal(key, shape, jnp.float32)
    if split:
        values = values * block_scale(key, shape, split, -0.22, 0.18)
    return jnp.clip(values, -limit, limit).astype(kind)


def setup_inputs(seed: int = 0) -> dict:
    seeds = jax.random.split(jax.random.key(seed), 7)
    queries = draw_queries(jax.random.fold_in(seeds[6], 71), 0)
    fresh_kv = bell_draw(seeds[1], (LAYERS, SPAN, KVH * 2 * HEAD), 1.0, 6.0, ((0, 64), (1, 8)))
    pool_kv = bell_draw(seeds[2], (OWNERS, POOL, PAGE, KVH * 2 * HEAD), 1.0, 6.0, ((0, 64), (3, 8)))
    hit_pages = plant(jax.random.randint(seeds[3], (LAYERS, HITS), 0, POOL), jax.random.fold_in(seeds[3], 1), 0, POOL - 1).astype(jnp.int32)
    hit_owners_keys = jax.random.split(jax.random.fold_in(seeds[4], 1), LAYERS * HITS // HITS)
    hit_owners_turns = jax.random.permutation(jax.random.fold_in(seeds[4], 3), LAYERS * HITS // HITS)
    hit_owners = jax.vmap(lambda own, number: shared_out(jax.random.fold_in(seeds[4], 2), own, number, HITS, N_SECTION, 1, MOST, 2))(hit_owners_keys, hit_owners_turns).reshape((LAYERS, HITS, 1))
    offsets = plant(jax.random.randint(seeds[5], (LAYERS,), PAGE, HITS * PAGE + 1), jax.random.fold_in(seeds[5], 1), PAGE, HITS * PAGE).astype(jnp.int32)
    return dict(queries=queries, fresh_kv=fresh_kv, pool_kv=pool_kv, hit_pages=hit_pages, hit_owners=hit_owners, offsets=offsets)


def visible_mask(start_pos):
    prefix = jnp.arange(HITS * PAGE) < start_pos
    prefix = jnp.broadcast_to(prefix[None, :], (SPAN, HITS * PAGE))
    causal = jnp.arange(SPAN)[None, :] <= jnp.arange(SPAN)[:, None]
    return jnp.concatenate([prefix, causal], axis=1)


def head_attention(query_rows, key_rows, values, visible):
    scores = jnp.dot(query_rows, key_rows.T, preferred_element_type=jnp.float32) * (HEAD ** -0.5)
    scores = jnp.where(visible, scores, jnp.float32(-1e30))
    row_max = jnp.max(scores, axis=1, keepdims=True)
    weights = jnp.where(visible, jnp.exp(scores - row_max), jnp.float32(0.0))
    row_sum = jnp.sum(weights, axis=1, keepdims=True)
    blended = jnp.dot(weights.astype(jnp.bfloat16), values, preferred_element_type=jnp.float32) / row_sum
    return blended.astype(jnp.bfloat16)


def reference(queries, fresh_kv, pool_kv, hit_pages, hit_owners, offsets):
    def one_layer(inputs):
        layer_q, layer_fresh, page_ids, owners_of, start_pos = inputs
        fetched = pool_kv[owners_of, page_ids].reshape(HITS * PAGE, KVH, 2 * HEAD)
        stacked = jnp.concatenate([fetched, layer_fresh.reshape(SPAN, KVH, 2 * HEAD)], axis=0)
        visible = visible_mask(start_pos)
        per_head = layer_q.reshape(SPAN, QH, HEAD).transpose(1, 0, 2)
        kv_groups = (jnp.arange(QH) // QPK).astype(jnp.int32)

        def one_head(head_item):
            query_rows, kv_group = head_item
            kv_pair = lax.dynamic_index_in_dim(stacked, kv_group, 1, keepdims=False)
            return head_attention(query_rows, kv_pair[:, :HEAD], kv_pair[:, HEAD:], visible)

        blended = lax.map(one_head, (per_head, kv_groups))
        return blended.transpose(1, 0, 2).reshape(SPAN, QH * HEAD)

    return lax.map(one_layer, (queries, fresh_kv, hit_pages, hit_owners[:, :, 0], offsets))
```

```python
import math

import jax
import jax.numpy as jnp
from jax import lax
from jax.experimental import pallas as pl
from jax.experimental.pallas import tpu as pltpu
from jax.sharding import PartitionSpec as P

HEAD = 128
HEADS = 8
PAGE = 64
MASKED = -1e30
TO_LOG2 = HEAD ** (-0.5) * math.log2(math.e)
FULL = 32767.0

MESH = pl.DeviceIdType.MESH
X_UP, X_DOWN = (1, 0, 0, 0), (3, 0, 0, 0)
Z_UP, Z_DOWN, Z_FAR = (0, 0, 1, 0), (0, 0, 15, 0), (0, 0, 8, 0)
Y_AWAY = [(0, d, 0, 0) for d in (1, 2, 3)]
CORE = (0, 0, 0, 1)


def place():
    section, z_lo = lax.axis_index("section"), lax.axis_index("tp")
    return section // 16, (section // 4) % 4, ((section // 2) % 2) * 8 + z_lo, section % 2


def device(delta):
    x, y, z, core = place()
    x, y, z, core = (x + delta[0]) % 4, (y + delta[1]) % 4, (z + delta[2]) % 16, (core + delta[3]) % 2
    return ((x * 4 + y) * 2 + z // 8) * 2 + core, z % 8


def remote(source, target, send, arrive, where):
    return pltpu.make_async_remote_copy(
        src_ref=source,
        dst_ref=target,
        send_sem=send,
        recv_sem=arrive,
        device_id=where,
        device_id_type=MESH,
    )


def column(row, size):
    down = lax.broadcasted_iota(jnp.int32, (size, size), 0)
    along = lax.broadcasted_iota(jnp.int32, (size, size), 1)
    return jnp.sum(jnp.where(down == along, row, 0), axis=1, keepdims=True)


def slot_table(pages, owners, offset):
    hits = pages.shape[1]
    down = lax.broadcasted_iota(jnp.int32, (hits, hits), 0)
    along = lax.broadcasted_iota(jnp.int32, (hits, hits), 1)
    owner_column = column(owners, hits)
    page_column = column(pages, hits)
    same = jnp.logical_and(owner_column == owners, along < down)
    rank = jnp.sum(jnp.where(same, 1, 0), axis=1, keepdims=True)
    slot = owner_column * 2 + rank
    match = slot == lax.broadcasted_iota(jnp.int32, (hits, 128), 1)
    first = lax.broadcasted_iota(jnp.int32, (hits, 128), 0) * PAGE
    rows = jnp.clip(offset - first, 0, PAGE)
    page_of = jnp.sum(jnp.where(match, page_column, 0), axis=0, keepdims=True)
    rows_of = jnp.sum(jnp.where(match, rows, 0), axis=0, keepdims=True)
    return page_of, rows_of


def coded(blend, low=1e-30):
    top = jnp.maximum(jnp.max(jnp.abs(blend), axis=0, keepdims=True), low)
    return jnp.round(blend * (FULL / top)).astype(jnp.int32).astype(jnp.int16), top * (1.0 / FULL)


def kernel(
    offset_ref, queries_ref, fresh_ref, pages_ref, owners_ref, pool_ref, out_ref,
    pool_00, pool_01, pool_10, pool_11, pool_20, pool_21, pool_30, pool_31, query_hops, query_all, table, table_s, fresh, keys, values_t, unit,
    part, part_stat, arrived, arrived_stat, back_hops, back_stat, back_stat_in,
    total, top_all, sum_all,
    local_sem, pool_send, pool_recv, core_send, core_recv, hop_send, hop_recv,
    spread_send, spread_recv, table_send, table_recv, fresh_send, fresh_recv,
    part_send, part_recv, stat_send, stat_recv, back_send, back_recv, home_send, home_recv,
):
    pools = ((pool_00, pool_01), (pool_10, pool_11), (pool_20, pool_21), (pool_30, pool_31))
    x, y, z, core = place()
    z_lo = lax.axis_index("tp")
    section = lax.axis_index("section")

    def tp_device(step):
        return section, (z_lo + step) % 8

    barrier = pltpu.get_barrier_semaphore()
    partners = [device(d) for d in [Z_FAR, Z_UP, Z_DOWN, X_UP, X_DOWN, CORE] + Y_AWAY]
    partners += [tp_device(step) for step in range(1, 8)]
    for partner in partners:
        pl.semaphore_signal(barrier, inc=1, device_id=partner, device_id_type=MESH)

    own_pool = pltpu.make_async_copy(pool_ref.at[0], pool_00, local_sem.at[0])
    own_pool.start()
    for h in range(HEADS):
        turned = queries_ref[0, :, h * HEAD:(h + 1) * HEAD].T
        query_hops[0, h] = turned
        query_all[0, 0, h] = turned
    page_of, rows_of = slot_table(pages_ref[...], owners_ref[...], offset_ref[0])
    table[0, 0, 0:1] = page_of
    table[0, 0, 1:2] = rows_of
    fresh[z_lo] = fresh_ref[0, :, pl.ds(pl.multiple_of(z_lo * 256, 256), 256)]
    first_row = lax.broadcasted_iota(jnp.int32, (128, 256), 0) == 0
    unit[...] = jnp.where(first_row, 1.0, 0.0).astype(jnp.bfloat16)
    own_pool.wait()

    pl.semaphore_wait(barrier, len(partners))

    def query_hop(step, h):
        return remote(
            query_hops.at[step, h], query_hops.at[step + 1, h],
            hop_send.at[step, h], hop_recv.at[step, h], device((Z_UP, Z_DOWN)[h % 2]),
        )

    def spread(group, h, away):
        source = query_hops.at[0 if group == 0 else 8, pl.ds(h, 2)]
        return remote(
            source, query_all.at[group, 4 - away, pl.ds(h, 2)],
            spread_send.at[group, away - 1, h // 2], spread_recv.at[group, away - 1, h // 2],
            device((0, away, 0, 0)),
        )

    def table_spread(group, away):
        return remote(
            table.at[group, 0], table.at[group, 4 - away],
            table_send.at[group, away - 1], table_recv.at[group, away - 1], device((0, away, 0, 0)),
        )

    for h in range(HEADS):
        query_hop(0, h).start()
    table_far = remote(table.at[0, 0], table.at[1, 0], table_send.at[2, 0], table_recv.at[2, 0], device(Z_FAR))
    table_far.start()
    low, high = pl.ds(0, 16), pl.ds(16, 16)
    mine = pool_00
    up_low = remote(mine.at[low], pool_10.at[low], pool_send.at[0], pool_recv.at[0], device(X_UP))
    down_high = remote(mine.at[high], pool_30.at[high], pool_send.at[1], pool_recv.at[1], device(X_DOWN))
    up_high = remote(mine.at[high], pool_10.at[high], pool_send.at[2], pool_recv.at[2], device(X_UP))
    down_low = remote(mine.at[low], pool_30.at[low], pool_send.at[3], pool_recv.at[3], device(X_DOWN))
    over_low = remote(pool_10.at[low], pool_20.at[low], pool_send.at[4], pool_recv.at[4], device(X_UP))
    over_high = remote(pool_30.at[high], pool_20.at[high], pool_send.at[5], pool_recv.at[5], device(X_DOWN))
    for copy in (up_low, down_high, up_high, down_low):
        copy.start()

    def across(chip):
        return remote(
            pools[chip][0], pools[chip][1], core_send.at[chip], core_recv.at[chip], device(CORE)
        )

    across(0).start()
    for away in (1, 2, 3):
        table_spread(0, away).start()
    fresh_copies = []
    for step in range(1, 8):
        columns = pl.ds(pl.multiple_of(((z_lo + step) % 8) * 256, 256), 256)
        copy = remote(
            fresh_ref.at[0, :, columns], fresh.at[z_lo],
            fresh_send.at[step - 1], fresh_recv.at[step - 1], tp_device(step),
        )
        copy.start()
        fresh_copies.append(copy)
    for h in range(0, HEADS, 2):
        for away in (1, 2, 3):
            spread(0, h, away).start()

    def query_step(step):
        for h in range(HEADS):
            query_hop(step - 1, h).wait_recv()
            query_hop(step, h).start()

    query_step(1)
    query_step(2)
    table_far.wait_recv()
    for away in (1, 2, 3):
        table_spread(1, away).start()
    query_step(3)

    for copy in fresh_copies:
        copy.wait_recv()
    fresh_all = fresh[...].reshape(128, 256)
    fresh_keys, fresh_values_t = fresh_all[:, :HEAD], fresh_all[:, HEAD:].T
    key_at = lax.broadcasted_iota(jnp.int32, (128, 128), 0)
    row_at = lax.broadcasted_iota(jnp.int32, (128, 128), 1)
    for h in range(HEADS):
        scores = jnp.dot(fresh_keys, query_all[0, 0, h], preferred_element_type=jnp.float32)
        scores = jnp.where(key_at <= row_at, scores, MASKED)
        top = jnp.max(scores, axis=0, keepdims=True)
        weights = jnp.exp2((scores - top) * TO_LOG2)
        total[h] = jnp.dot(fresh_values_t, weights.astype(jnp.bfloat16), preferred_element_type=jnp.float32)
        top_all[h] = top * TO_LOG2
        sum_all[h] = jnp.sum(weights, axis=0, keepdims=True)

    query_step(4)
    up_low.wait_recv()
    over_low.start()
    down_high.wait_recv()
    over_high.start()
    for step in (5, 6, 7):
        query_step(step)
    for h in range(HEADS):
        query_hop(7, h).wait_recv()
        query_all[1, 0, h] = query_hops[8, h]
        if h % 2:
            for away in (1, 2, 3):
                spread(1, h - 1, away).start()

    for group in (0, 1):
        for away in (1, 2, 3):
            table_spread(group, away).wait_recv()
    to_scalar = pltpu.make_async_copy(table, table_s, local_sem.at[1])
    to_scalar.start()
    to_scalar.wait()

    lane = lax.broadcasted_iota(jnp.int32, (128, 128), 1)
    sublane = lax.broadcasted_iota(jnp.int32, (128, 128), 0)

    def lay_out(chip, side):
        owner = ((((x - chip + 4) % 4) * 4 + y) * 2 + z // 8) * 2 + (core + side) % 2
        at = (chip * 2 + side) * 128

        def one(layer, carry):
            group, near = layer // 4, layer % 4
            page_0, page_1 = table_s[group, near, 0, owner * 2], table_s[group, near, 0, owner * 2 + 1]
            rows_0, rows_1 = table_s[group, near, 1, owner * 2], table_s[group, near, 1, owner * 2 + 1]
            both = jnp.concatenate([pools[chip][side][page_0], pools[chip][side][page_1]], axis=0)
            keys[layer, at:at + 128, :HEAD] = both[:, :HEAD]
            values_t[layer, :, at:at + 128] = both[:, HEAD:].T
            seen = jnp.where(sublane < PAGE, rows_0 - sublane, rows_1 + PAGE - sublane) > 0
            hidden = jnp.logical_and(lane == 0, jnp.logical_not(seen))
            keys[layer, at:at + 128, HEAD:] = jnp.where(hidden, MASKED, 0.0).astype(jnp.bfloat16)
            return carry

        lax.fori_loop(0, 8, one, 0)

    lay_out(0, 0)
    up_high.wait_recv()
    across(1).start()
    lay_out(1, 0)
    down_low.wait_recv()
    across(3).start()
    lay_out(3, 0)
    for chip in (0, 1, 3):
        across(chip).wait_recv()
        lay_out(chip, 1)
    over_low.wait_recv()
    over_high.wait_recv()
    across(2).start()
    lay_out(2, 0)
    across(2).wait_recv()
    lay_out(2, 1)

    def partial(group, near, pair):
        layer = group * 4 + near
        heads = jnp.concatenate([query_all[group, near, 2 * pair], query_all[group, near, 2 * pair + 1]], axis=1)
        right = jnp.concatenate([heads, unit[...]], axis=0)
        scores = jnp.dot(keys[layer], right, preferred_element_type=jnp.float32)
        top = jnp.max(scores, axis=0, keepdims=True)
        weights = jnp.exp2((scores - top) * TO_LOG2)
        row_sum = jnp.sum(weights, axis=0, keepdims=True)
        blend = jnp.dot(values_t[layer], weights.astype(jnp.bfloat16), preferred_element_type=jnp.float32)
        code, scale = coded(blend)
        scale = scale / row_sum
        level = top * TO_LOG2 + jnp.log2(row_sum)
        for i in (0, 1):
            cut = slice(i * 128, (i + 1) * 128)
            part[group, near, 2 * pair + i] = code[:, cut]
            part_stat[group, near, 2 * pair + i, 0:1] = level[:, cut]
            part_stat[group, near, 2 * pair + i, 1:2] = scale[:, cut]

    def send_part(group, near, pair):
        heads = pl.ds(2 * pair, 2)
        return remote(
            part.at[group, near, heads], arrived.at[group, 3 - near, heads],
            part_send.at[group, near - 1, pair], part_recv.at[group, near - 1, pair], device((0, near, 0, 0)),
        )

    def send_stat(group, near, pair):
        heads = pl.ds(2 * pair, 2)
        return remote(
            part_stat.at[group, near, heads], arrived_stat.at[group, 3 - near, heads],
            stat_send.at[group, near - 1, pair], stat_recv.at[group, near - 1, pair], device((0, near, 0, 0)),
        )

    def partials(group, pair):
        def one(near, carry):
            partial(group, near, pair)
            return carry

        lax.fori_loop(0, 4, one, 0)
        for near in (1, 2, 3):
            send_part(group, near, pair).start()
            send_stat(group, near, pair).start()

    def received(group, pair):
        for near in (1, 2, 3):
            send_part(group, near, pair).wait_recv()
            send_stat(group, near, pair).wait_recv()

    def merged(group, h):
        codes = [part[group, 0, h]] + [arrived[group, i, h] for i in range(3)]
        stats = [part_stat[group, 0, h]] + [arrived_stat[group, i, h] for i in range(3)]
        top = stats[0][0:1]
        for stat in stats[1:]:
            top = jnp.maximum(top, stat[0:1])
        shares = [jnp.exp2(stat[0:1] - top) for stat in stats]
        row_sum = shares[0] + shares[1] + shares[2] + shares[3]
        blend = None
        for code, stat, share in zip(codes, stats, shares):
            term = code.astype(jnp.int32).astype(jnp.float32) * (share * stat[1:2])
            blend = term if blend is None else blend + term
        return blend, top, row_sum

    def back_hop(step, h):
        return remote(
            back_hops.at[step, h], back_hops.at[step + 1, h],
            back_send.at[step, h], back_recv.at[step, h], device((Z_UP, Z_DOWN)[h % 2]),
        )

    def home(pair):
        heads = pl.ds(2 * pair, 2)
        return remote(
            back_stat.at[heads], back_stat_in.at[heads], home_send.at[pair], home_recv.at[pair], device(Z_FAR)
        )

    for h in range(0, HEADS, 2):
        for away in (1, 2, 3):
            spread(1, h, away).wait_recv()
            spread(0, h, away).wait_recv()
    lax.fori_loop(0, 4, lambda pair, carry: (partials(1, pair), carry)[1], 0)
    for pair in range(4):
        received(1, pair)
        for i in (0, 1):
            h = 2 * pair + i
            blend, top, row_sum = merged(1, h)
            code, scale = coded(blend)
            back_hops[0, h] = code
            back_stat[h, 0:1] = top + jnp.log2(row_sum)
            back_stat[h, 1:2] = scale / row_sum
            back_hop(0, h).start()
        home(pair).start()

    def back_step(step):
        for h in range(HEADS):
            back_hop(step - 1, h).wait_recv()
            back_hop(step, h).start()

    def include(h, blend, top, row_sum):
        new = jnp.maximum(top_all[h], top)
        old_share, share = jnp.exp2(top_all[h] - new), jnp.exp2(top - new)
        total[h] = total[h] * old_share + blend * share
        sum_all[h] = sum_all[h] * old_share + row_sum * share
        top_all[h] = new

    for pair in range(4):
        partials(0, pair)
        back_step(pair + 1)
    for pair in range(4):
        received(0, pair)
        for h in (2 * pair, 2 * pair + 1):
            blend, top, row_sum = merged(0, h)
            include(h, blend, top, row_sum)
        if pair < 3:
            back_step(pair + 5)
    for pair in range(4):
        home(pair).wait_recv()
        for h in (2 * pair, 2 * pair + 1):
            back_hop(7, h).wait_recv()
            stat = back_stat_in[h]
            blend = back_hops[8, h].astype(jnp.int32).astype(jnp.float32) * stat[1:2]
            include(h, blend, stat[0:1], jnp.ones_like(stat[0:1]))
            result = total[h] / sum_all[h]
            out_ref[0, :, h * HEAD:(h + 1) * HEAD] = result.T.astype(jnp.bfloat16)

    for step in range(8):
        for h in range(HEADS):
            query_hop(step, h).wait_send()
            back_hop(step, h).wait_send()
    for copy in [up_low, up_high, down_low, down_high, over_low, over_high, table_far] + fresh_copies:
        copy.wait_send()
    for chip in range(4):
        across(chip).wait_send()
    for pair in range(4):
        home(pair).wait_send()
    for group in (0, 1):
        for away in (1, 2, 3):
            table_spread(group, away).wait_send()
            for pair in range(4):
                spread(group, 2 * pair, away).wait_send()
                send_part(group, away, pair).wait_send()
                send_stat(group, away, pair).wait_send()


def local(queries, fresh_kv, pool_kv, hit_pages, hit_owners, offsets):
    bf16, i16, f32 = jnp.bfloat16, jnp.int16, jnp.float32
    vmem, dma = pltpu.VMEM, pltpu.SemaphoreType.DMA
    in_vmem = pl.BlockSpec(memory_space=pltpu.VMEM)
    scratch = [
        *[vmem((32, PAGE, 256), bf16) for _ in range(8)],
        vmem((9, HEADS, HEAD, 128), bf16),
        vmem((2, 4, HEADS, HEAD, 128), bf16),
        vmem((2, 4, 2, 128), jnp.int32),
        pltpu.SMEM((2, 4, 2, 128), jnp.int32),
        vmem((8, 16, 256), bf16),
        vmem((8, 1024, 256), bf16),
        vmem((8, HEAD, 1024), bf16),
        vmem((128, 256), bf16),
        vmem((2, 4, HEADS, HEAD, 128), i16),
        vmem((2, 4, HEADS, 2, 128), f32),
        vmem((2, 3, HEADS, HEAD, 128), i16),
        vmem((2, 3, HEADS, 2, 128), f32),
        vmem((9, HEADS, HEAD, 128), i16),
        vmem((HEADS, 2, 128), f32),
        vmem((HEADS, 2, 128), f32),
        vmem((HEADS, HEAD, 128), f32),
        vmem((HEADS, 1, 128), f32),
        vmem((HEADS, 1, 128), f32),
        dma((2,)),
        dma((6,)), dma((6,)),
        dma((4,)), dma((4,)),
        dma((8, HEADS)), dma((8, HEADS)),
        dma((2, 3, 4)), dma((2, 3, 4)),
        dma((3, 3)), dma((3, 3)),
        dma((7,)), dma((7,)),
        dma((2, 3, 4)), dma((2, 3, 4)),
        dma((2, 3, 4)), dma((2, 3, 4)),
        dma((8, HEADS)), dma((8, HEADS)),
        dma((4,)), dma((4,)),
    ]
    return pl.pallas_call(
        kernel,
        out_shape=jax.ShapeDtypeStruct(queries.shape, queries.dtype),
        in_specs=[
            pl.BlockSpec(memory_space=pltpu.SMEM), in_vmem, in_vmem, in_vmem, in_vmem,
            pl.BlockSpec(memory_space=pl.ANY),
        ],
        out_specs=in_vmem,
        scratch_shapes=scratch,
        name="spanned_attention",
        compiler_params=pltpu.CompilerParams(
            collective_id=0, has_side_effects=True, vmem_limit_bytes=56 << 20
        ),
    )(offsets, queries, fresh_kv, hit_pages, hit_owners.reshape(1, -1), pool_kv)


def solution(mesh):
    return jax.shard_map(
        local,
        mesh=mesh,
        in_specs=(
            P("section", None, "tp"),
            P("section", "tp", None),
            P("section", None, None, "tp"),
            P("section", None),
            P("section", None, None),
            P("section"),
        ),
        out_specs=P("section", None, "tp"),
        check_vma=False,
    )
```
